32 devices in a mesh: dp: 4 (over y, x), cent: 8 (over z, core).
Axes of the slice: x: 2, y: 2, z: 4, core: 2. Of those that a mesh axis runs over, the one named last changes fastest.
Arguments:
- points: bfloat16 [4096, 768], P('dp'), may hold values from -16 to 16
- centroids: bfloat16 [16384, 768], P(('cent', 'dp')), may hold values from -24 to 24
Outputs:
- newest: bfloat16 [16384, 768], P(('cent', 'dp'))
- previous: bfloat16 [16384, 768], P(('cent', 'dp'))
- row_potential: float32 [4096], P('dp')
- list_potential: float32 [16384], P(('cent', 'dp'))
The draws below stay inside these ranges and needn't reach their ends.
All inputs are finite; a program needn't handle non-finite values.
Results may differ from the reference program's by a relative error of at most 0.011.
Values may be sent and summed in bfloat16 or wider, within the bound.
A program may use at most 128 MiB of HBM per device.

```python
import math
import jax
import jax.numpy as jnp
from jax import lax

D = 768
K_DEV = 2048
ITERS = 3
ROWS = 4096
LISTS = 16384


def centroid_base(key):
    return jnp.clip(jax.random.normal(key, (LISTS, D), jnp.float32), -4.0, 4.0)


def draw_points(key, part):
    key = jax.random.fold_in(key, 11)
    first = jax.random.fold_in(key, 0)
    drawn = jnp.clip(jax.random.normal(first, (ROWS, D), jnp.float32), -5.0, 5.0)
    return drawn.astype(jnp.bfloat16)


def draw_centroids(key, part):
    base = centroid_base(key)
    result = base
    return result.astype(jnp.bfloat16)


def setup_inputs(seed: int = 0) -> dict:
    arg_keys = jax.random.split(jax.random.key(seed), 3)
    return {
        "points": draw_points(jax.random.fold_in(arg_keys[2], 71), 0),
        "centroids": draw_centroids(jax.random.fold_in(arg_keys[2], 71), 0),
    }


sharpness = 4.0

def scores_of(points, block):
    product = lax.dot_general(points, block, (((1,), (1,)), ((), ())), preferred_element_type=jnp.float32)
    return sharpness / math.sqrt(D) * product

def reference(points, centroids):
    log_ratio = math.log(ROWS / LISTS)
    prior = 0.5 * ROWS / LISTS
    history = [centroids]
    row_pot = jnp.zeros((ROWS,), jnp.float32)
    col_pot = jnp.zeros((LISTS,), jnp.float32)
    for step in range(ITERS):
        used = history[max(step - 1, 0)]
        blocks = used.reshape(LISTS // K_DEV, K_DEV, D)

        def first_pass(carry, block):
            top, total = carry
            logits = scores_of(points, block)
            shifted = logits + row_pot[:, None]
            cmax = lax.optimization_barrier(jnp.max(shifted, axis=0))
            cpot = log_ratio - (cmax + jnp.log(lax.optimization_barrier(jnp.sum(jnp.exp(shifted - cmax[None, :]), axis=0))))
            inner = logits + cpot[None, :]
            rmax = lax.optimization_barrier(jnp.max(inner, axis=1))
            rsum = lax.optimization_barrier(jnp.sum(jnp.exp(inner - rmax[:, None]), axis=1))
            newtop = jnp.maximum(top, rmax)
            newtotal = total * jnp.exp(top - newtop) + rsum * jnp.exp(rmax - newtop)
            return ((newtop, newtotal), cpot)
        start = (jnp.full((ROWS,), -jnp.inf, jnp.float32), jnp.zeros((ROWS,), jnp.float32))
        (top, total), cpots = lax.scan(first_pass, start, blocks)
        col_pot = cpots.reshape(LISTS)
        row_pot = -(top + jnp.log(total))
        current_rows = row_pot

        def second_pass(inputs):
            block, cpot = inputs
            logits = scores_of(points, block)
            plan = jnp.exp(logits + current_rows[:, None] + cpot[None, :])
            mass = lax.optimization_barrier(jnp.sum(plan, axis=0))
            weighted = lax.dot_general(plan.astype(jnp.bfloat16), points, (((0,), (0,)), ((), ())), preferred_element_type=jnp.float32)
            fresh = (weighted + prior * block.astype(jnp.float32)) / (mass + prior)[:, None]
            return fresh.astype(jnp.bfloat16)
        fresh = lax.map(second_pass, (blocks, cpots))
        history.append(fresh.reshape(LISTS, D))
    return (history[-1], history[-2], row_pot, col_pot)
```

```python
import functools
import math

import jax
import jax.numpy as jnp
from jax import lax
from jax.experimental import pallas as pl
from jax.experimental.pallas import tpu as pltpu
from jax.sharding import PartitionSpec as P

sharpness = 4.0
LANES = 128
LOG2E = math.log2(math.e)
LN2 = math.log(2.0)


def flip(i, bit):
    return i + bit - 2 * bit * ((i // bit) % 2)


def tile_lanes(col, width):
    return jnp.concatenate([col] * (width // LANES), axis=1)


def lane_groups(x):
    return [x[:, g : g + LANES] for g in range(0, x.shape[1], LANES)]


def fold(op, parts):
    return functools.reduce(op, parts)


def sub8(op, x):
    return fold(op, [x[g : g + 8] for g in range(0, x.shape[0], 8)])


def kernel(
    n_dp, n_cent,
    pts_in, cen,
    newest, previous, row_out, list_out,
    pts, lt, lt2, pb, acc, c1, top, tot, cp, ratio_j, mass, row_a, row_b, row_m,
    mine, gathered, full,
    own_sem, ag_send, ag_recv, sib_send, sib_recv, x1_send, x1_recv, x2_send, x2_recv,
):
    n = n_dp * n_cent
    _, blk, width = pts_in.shape
    nb = 2 * n_dp
    lists = cen.shape[0]
    rows_all = nb * blk
    w_all = rows_all // LANES
    per = blk // LANES
    quarter = blk // 2
    log_ratio = math.log2(rows_all / (lists * n))
    prior = 0.5 * rows_all / (lists * n)
    factor = sharpness / math.sqrt(width) * LOG2E
    strip = 64
    strips = [pl.ds(s, strip) for s in range(0, lists, strip)]

    d = lax.axis_index("dp")
    k = lax.axis_index("cent")
    core = lax.rem(k, 2)
    sib = flip(k, 1)
    me = k * n_dp + d
    my_w = lax.rem(me, w_all)

    def dev(e):
        return {"dp": lax.rem(e, n_dp), "cent": e // n_dp}

    barrier = pltpu.get_barrier_semaphore()

    def greet(o, _):
        e = lax.rem(me + o, n)
        pl.semaphore_signal(barrier, inc=1, device_id=dev(e), device_id_type=pl.DeviceIdType.MESH)
        return 0

    lax.fori_loop(1, n, greet, 0)
    own_copy = pltpu.make_async_copy(pts_in, pts.at[pl.ds(2 * d, 2)], own_sem)
    own_copy.start()
    top[...] = jnp.full_like(top, -jnp.inf)
    tot[...] = jnp.zeros_like(tot)
    pl.semaphore_wait(barrier, n - 1)

    def remote(src, dst, ss, rs, to):
        return pltpu.make_async_remote_copy(
            src_ref=src, dst_ref=dst, send_sem=ss, recv_sem=rs,
            device_id=to, device_id_type=pl.DeviceIdType.MESH,
        )

    def online(x, s):
        groups = lane_groups(x)
        old = top[s, :]
        new = jnp.maximum(old, fold(jnp.maximum, groups))
        tot[s, :] = tot[s, :] * jnp.exp2(old - new) + fold(
            jnp.add, [jnp.exp2(g - new) for g in groups]
        )
        top[s, :] = new

    def dot_scores(c_ref, i, out):
        for q in range(2):
            lanes = pl.ds(q * quarter, quarter)
            out[i, :, lanes] = factor * lax.dot_general(
                c_ref[...], pts[i, lanes, :], (((1,), (1,)), ((), ())),
                preferred_element_type=jnp.float32,
            )

    def first_scores(i):
        dot_scores(cen, i, lt)
        for s in strips:
            online(lt[i, s, :], s)

    def many_scores(blocks):
        def body(t, _):
            i = blocks[0]
            for u in range(1, len(blocks)):
                i = jnp.where(t == u, blocks[u], i)
            first_scores(i)
            return 0

        lax.fori_loop(0, len(blocks), body, 0)

    def forward(slot, j, rows):
        ref = pts.at[j, rows]
        cp_ = remote(ref, ref, sib_send.at[slot], sib_recv.at[slot], {"dp": d, "cent": sib})
        cp_.start()
        return cp_

    pending = []
    if n_dp == 4:
        dx, dy = flip(d, 1), flip(d, 2)
        dd = flip(dx, 2)
        part = (pl.ds(0, quarter), pl.ds(quarter, quarter))
        hx, hy, hd, ho = 2 * dx + core, 2 * dy + core, 2 * dd + core, 2 * d + core
        to_x, to_y = {"dp": dx, "cent": k}, {"dp": dy, "cent": k}

        def own_send(slot, p, to):
            c = remote(pts_in.at[core, part[p]], pts.at[ho, part[p]], ag_send.at[slot], ag_recv.at[slot], to)
            c.start()
            return c

        def relay(slot, j, p, to):
            ref = pts.at[j, part[p]]
            c = remote(ref, ref, ag_send.at[slot], ag_recv.at[slot], to)
            c.start()
            return c

        s0 = own_send(0, 1, to_x)
        s3 = own_send(3, 0, to_y)
        s1 = own_send(1, 0, to_x)
        s4 = own_send(4, 1, to_y)
        own_copy.wait()
        many_scores([2 * d, 2 * d + 1])
        s3.wait_recv()
        s2 = relay(2, hy, 0, to_x)
        f0 = forward(0, hy, part[0])
        s0.wait_recv()
        s5 = relay(5, hx, 1, to_y)
        f1 = forward(1, hx, part[1])
        s1.wait_recv()
        f2 = forward(2, hx, part[0])
        s4.wait_recv()
        f3 = forward(3, hy, part[1])
        many_scores([hx, hy])
        for f in (f0, f1, f2, f3):
            f.wait_recv()
        many_scores([flip(hx, 1), flip(hy, 1)])
        s2.wait_recv()
        f4 = forward(4, hd, part[0])
        s5.wait_recv()
        f5 = forward(5, hd, part[1])
        many_scores([hd])
        f4.wait_recv()
        f5.wait_recv()
        many_scores([flip(hd, 1)])
        pending = [s0, s1, s2, s3, s4, s5, f0, f1, f2, f3, f4, f5]
    else:
        sends = []
        for o in range(1, n_dp):
            c = remote(
                pts_in.at[core], pts.at[2 * d + core], ag_send.at[o - 1], ag_recv.at[o - 1],
                {"dp": lax.rem(d + o, n_dp), "cent": k},
            )
            c.start()
            sends.append(c)
        own_copy.wait()
        many_scores([2 * d, 2 * d + 1])
        forwards = []
        for o in range(1, n_dp):
            sends[o - 1].wait_recv()
            j = 2 * lax.rem(d + n_dp - o, n_dp) + core
            forwards.append(forward(o - 1, j, pl.ds(0, blk)))
        for o in range(1, n_dp):
            j = 2 * lax.rem(d + n_dp - o, n_dp) + core
            many_scores([j])
            forwards[o - 1].wait_recv()
            many_scores([flip(j, 1)])
        pending = sends + forwards
    for c in pending:
        c.wait_send()

    def finish_columns():
        for s in strips:
            t = top[s, :]
            m = jnp.max(t, axis=1, keepdims=True)
            total = jnp.sum(tot[s, :] * jnp.exp2(t - m), axis=1, keepdims=True)
            cp[s, :] = jnp.broadcast_to(log_ratio - (m + jnp.log2(total)), (strip, LANES))

    def put_chunks(x, i, v):
        for g in range(per):
            mine[x, i * per + g] = v[:, g * LANES : (g + 1) * LANES]

    def row_pass(ref, x):
        def body(i, _):
            def inner(s):
                return ref[i, s, :] + tile_lanes(cp[s, :], blk)

            m8 = fold(jnp.maximum, [sub8(jnp.maximum, inner(s)) for s in strips])
            rmax = jnp.max(m8, axis=0, keepdims=True)
            part_sum = None
            for s in strips:
                e = jnp.exp2(inner(s) - rmax)
                ref[i, s, :] = e
                t = sub8(jnp.add, e)
                part_sum = t if part_sum is None else part_sum + t
            total = jnp.sum(part_sum, axis=0, keepdims=True)
            row_m[i] = rmax
            put_chunks(x, i, rmax + jnp.log2(total))
            return 0

        lax.fori_loop(0, nb, body, 0)

    def start_exchange(x):
        def send(o, _):
            e = lax.rem(me + o, n)
            remote(
                mine.at[x, lax.rem(e, w_all)], gathered.at[x, me], x1_send.at[x], x1_recv.at[x], dev(e)
            ).start()
            return 0

        lax.fori_loop(1, n, send, 0)
        gathered[x, me] = mine[x, my_w]

    def wait_bytes(ref, sem):
        pltpu.make_async_copy(ref, ref, sem).wait()

    def middle_exchange(x, logs):
        wait_bytes(gathered.at[x, pl.ds(0, n - 1)], x1_recv.at[x])
        wait_bytes(gathered.at[x, pl.ds(0, n - 1)], x1_send.at[x])
        v = gathered[x]
        if logs:
            m = jnp.max(v, axis=0, keepdims=True)
            res = m + jnp.log2(jnp.sum(jnp.exp2(v - m), axis=0, keepdims=True))
        else:
            res = jnp.sum(v, axis=0, keepdims=True)
        full[x, my_w] = res[0]

        def send(o, _):
            e = (me // w_all) * w_all + lax.rem(my_w + o, w_all)
            ref = full.at[x, my_w]
            remote(ref, ref, x2_send.at[x], x2_recv.at[x], dev(e)).start()
            return 0

        lax.fori_loop(1, w_all, send, 0)

    def end_exchange(x):
        wait_bytes(full.at[x, pl.ds(0, w_all - 1)], x2_recv.at[x])
        wait_bytes(full.at[x, pl.ds(0, w_all - 1)], x2_send.at[x])

    def full_row(x, i):
        return jnp.concatenate([full[x, i * per + g] for g in range(per)], axis=1)

    def weigh(ref, scale_of):
        mass[...] = jnp.zeros_like(mass)
        acc[...] = jnp.zeros_like(acc)

        def body(i, _):
            scale = scale_of(i)
            for s in strips:
                p = ref[i, s, :] * scale
                mass[s, :] += fold(jnp.add, lane_groups(p))
                pb[s, :] = p.astype(jnp.bfloat16)
            acc[...] += jnp.dot(pb[...], pts[i], preferred_element_type=jnp.float32)
            return 0

        lax.fori_loop(0, nb, body, 0)

    def refresh(out, used, gain):
        for s in strips:
            m = jnp.sum(mass[s, :], axis=1, keepdims=True)
            wgt = acc[s, :]
            if gain:
                r = ratio_j[s, :][:, 0:1]
                m, wgt = m * r, wgt * r
            fresh = (wgt + prior * used[s, :].astype(jnp.float32)) / (m + prior)
            out[s, :] = fresh.astype(jnp.bfloat16)

    finish_columns()
    row_pass(lt, 0)
    start_exchange(0)
    middle_exchange(0, True)
    end_exchange(0)

    def scale_0(i):
        v = jnp.exp2(row_m[i] - full_row(0, i))
        row_a[i] = v
        return v

    weigh(lt, scale_0)
    refresh(c1, cen, False)
    for s in strips:
        m = jnp.sum(mass[s, :], axis=1, keepdims=True)
        ratio_j[s, :] = jnp.broadcast_to(2.0**log_ratio / m, (strip, LANES))

    def row_sums(i, _):
        part_sum = fold(
            jnp.add,
            [sub8(jnp.add, lt[i, s, :] * tile_lanes(ratio_j[s, :], blk)) for s in strips],
        )
        put_chunks(1, i, jnp.sum(part_sum, axis=0, keepdims=True) * row_a[i])
        return 0

    lax.fori_loop(0, nb, row_sums, 0)
    start_exchange(1)

    def second_scores(i, _):
        dot_scores(c1, i, lt2)
        return 0

    lax.fori_loop(0, nb // 2, second_scores, 0)
    middle_exchange(1, False)
    lax.fori_loop(nb // 2, nb, second_scores, 0)
    end_exchange(1)

    top[...] = jnp.full_like(top, -jnp.inf)
    tot[...] = jnp.zeros_like(tot)

    def second_columns(i, _):
        t = full_row(1, i)
        row_b[i] = row_a[i] / t
        pot = -full_row(0, i) - jnp.log2(t)
        for s in strips:
            online(lt2[i, s, :] + pot, s)
        return 0

    lax.fori_loop(0, nb, second_columns, 0)
    finish_columns()
    row_pass(lt2, 2)
    start_exchange(2)
    middle_exchange(2, True)
    weigh(lt, lambda i: row_b[i])
    refresh(previous, cen, True)
    end_exchange(2)
    weigh(lt2, lambda i: jnp.exp2(row_m[i] - full_row(2, i)))
    refresh(newest, c1, False)
    for h in range(2):
        row_out[h] = -LN2 * full_row(2, 2 * d + h)
    list_out[...] = LN2 * cp[...].T[0:1, :]


def shards(n_dp, n_cent, points, centroids):
    rows, width = points.shape
    lists = centroids.shape[0]
    n = n_dp * n_cent
    blk = rows // 2
    nb = 2 * n_dp
    w_all = rows * n_dp // LANES
    f32, bf16 = jnp.float32, jnp.bfloat16
    dma = pltpu.SemaphoreType.DMA
    vmem = pl.BlockSpec(memory_space=pltpu.VMEM)
    newest, previous, row_pot, list_pot = pl.pallas_call(
        functools.partial(kernel, n_dp, n_cent),
        out_shape=(
            jax.ShapeDtypeStruct((lists, width), bf16),
            jax.ShapeDtypeStruct((lists, width), bf16),
            jax.ShapeDtypeStruct((2, 1, blk), f32),
            jax.ShapeDtypeStruct((1, lists), f32),
        ),
        in_specs=[pl.BlockSpec(memory_space=pl.ANY), vmem],
        out_specs=(vmem, vmem, vmem, vmem),
        scratch_shapes=[
            pltpu.VMEM((nb, blk, width), bf16),
            pltpu.VMEM((nb, lists, blk), f32),
            pltpu.VMEM((nb, lists, blk), f32),
            pltpu.VMEM((lists, blk), bf16),
            pltpu.VMEM((lists, width), f32),
            pltpu.VMEM((lists, width), bf16),
            pltpu.VMEM((lists, LANES), f32),
            pltpu.VMEM((lists, LANES), f32),
            pltpu.VMEM((lists, LANES), f32),
            pltpu.VMEM((lists, LANES), f32),
            pltpu.VMEM((lists, LANES), f32),
            pltpu.VMEM((nb, 1, blk), f32),
            pltpu.VMEM((nb, 1, blk), f32),
            pltpu.VMEM((nb, 1, blk), f32),
            pltpu.VMEM((3, w_all, 1, LANES), f32),
            pltpu.VMEM((3, n, 1, LANES), f32),
            pltpu.VMEM((3, w_all, 1, LANES), f32),
            dma, dma((2 * n_dp,)), dma((2 * n_dp,)), dma((2 * n_dp,)), dma((2 * n_dp,)),
            dma((3,)), dma((3,)), dma((3,)), dma((3,)),
        ],
        compiler_params=pltpu.CompilerParams(
            collective_id=0, has_side_effects=True, vmem_limit_bytes=52 * 1024 * 1024
        ),
    )(points.reshape(2, blk, width), centroids)
    return newest, previous, row_pot.reshape(rows), list_pot.reshape(lists)


def solution(mesh):
    return jax.shard_map(
        functools.partial(shards, mesh.shape["dp"], mesh.shape["cent"]),
        mesh=mesh,
        in_specs=(P("dp", None), P(("cent", "dp"), None)),
        out_specs=(P(("cent", "dp"), None), P(("cent", "dp"), None), P("dp"), P(("cent", "dp"))),
        check_vma=False,
    )
```

```python
import functools
import math

import jax
import jax.numpy as jnp
from jax import lax
from jax.experimental import pallas as pl
from jax.experimental.pallas import tpu as pltpu
from jax.sharding import PartitionSpec as P

sharpness = 4.0
LANES = 128
LOG2E = math.log2(math.e)
LN2 = math.log(2.0)


def flip(i, bit):
    return i + bit - 2 * bit * ((i // bit) % 2)


def tile_lanes(col, width):
    return jnp.concatenate([col] * (width // LANES), axis=1)


def lane_groups(x):
    return [x[:, g : g + LANES] for g in range(0, x.shape[1], LANES)]


def fold(op, parts):
    return functools.reduce(op, parts)


def sub8(op, x):
    return fold(op, [x[g : g + 8] for g in range(0, x.shape[0], 8)])


def kernel(
    n_dp, n_cent,
    pts_in, cen,
    newest, previous, row_out, list_out,
    pts, lt, lt2, pb, acc, c1, top, tot, cp, ratio_j, mass, row_a, row_b, row_m,
    mine, gathered, full,
    own_sem, ag_send, ag_recv, sib_send, sib_recv, x1_send, x1_recv, x2_send, x2_recv,
):
    n = n_dp * n_cent
    _, blk, width = pts_in.shape
    nb = 2 * n_dp
    lists = cen.shape[0]
    rows_all = nb * blk
    w_all = rows_all // LANES
    per = blk // LANES
    quarter = blk // 2
    log_ratio = math.log2(rows_all / (lists * n))
    prior = 0.5 * rows_all / (lists * n)
    factor = sharpness / math.sqrt(width) * LOG2E
    strip = 64
    strips = [pl.ds(s, strip) for s in range(0, lists, strip)]

    d = lax.axis_index("dp")
    k = lax.axis_index("cent")
    core = lax.rem(k, 2)
    sib = flip(k, 1)
    me = k * n_dp + d
    my_w = lax.rem(me, w_all)
    w_half = w_all // 2
    my_half = my_w // w_half

    def dev(e):
        return {"dp": lax.rem(e, n_dp), "cent": e // n_dp}

    barrier = pltpu.get_barrier_semaphore()

    def greet(o, _):
        e = lax.rem(me + o, n)
        pl.semaphore_signal(barrier, inc=1, device_id=dev(e), device_id_type=pl.DeviceIdType.MESH)
        return 0

    lax.fori_loop(1, n, greet, 0)
    own_copy = pltpu.make_async_copy(pts_in, pts.at[pl.ds(2 * d, 2)], own_sem)
    own_copy.start()
    top[...] = jnp.full_like(top, -jnp.inf)
    tot[...] = jnp.zeros_like(tot)
    pl.semaphore_wait(barrier, n - 1)

    def remote(src, dst, ss, rs, to):
        return pltpu.make_async_remote_copy(
            src_ref=src, dst_ref=dst, send_sem=ss, recv_sem=rs,
            device_id=to, device_id_type=pl.DeviceIdType.MESH,
        )

    def online(x, s):
        groups = lane_groups(x)
        old = top[s, :]
        new = jnp.maximum(old, fold(jnp.maximum, groups))
        tot[s, :] = tot[s, :] * jnp.exp2(old - new) + fold(
            jnp.add, [jnp.exp2(g - new) for g in groups]
        )
        top[s, :] = new

    def dot_scores(c_ref, i, out):
        for q in range(2):
            lanes = pl.ds(q * quarter, quarter)
            out[i, :, lanes] = factor * lax.dot_general(
                c_ref[...], pts[i, lanes, :], (((1,), (1,)), ((), ())),
                preferred_element_type=jnp.float32,
            )

    def first_scores(i):
        dot_scores(cen, i, lt)
        for s in strips:
            online(lt[i, s, :], s)

    def many_scores(blocks):
        def body(t, _):
            i = blocks[0]
            for u in range(1, len(blocks)):
                i = jnp.where(t == u, blocks[u], i)
            first_scores(i)
            return 0

        lax.fori_loop(0, len(blocks), body, 0)

    def forward(slot, j, rows):
        ref = pts.at[j, rows]
        cp_ = remote(ref, ref, sib_send.at[slot], sib_recv.at[slot], {"dp": d, "cent": sib})
        cp_.start()
        return cp_

    pending = []
    if n_dp == 4 and n_cent % 4 == 0:
        dx, dy = flip(d, 1), flip(d, 2)
        dd = flip(dx, 2)
        hx, hy, hd, ho = 2 * dx + core, 2 * dy + core, 2 * dd + core, 2 * d + core
        to_x, to_y = {"dp": dx, "cent": k}, {"dp": dy, "cent": k}
        to_z = {"dp": d, "cent": flip(k, 2)}
        unit = blk // 4
        odd = lax.rem(k // 2, 2)
        first = pl.ds(pl.multiple_of(odd * 3 * unit, unit), unit)
        other = pl.ds(pl.multiple_of((1 - odd) * 3 * unit, unit), unit)
        q1, q2 = pl.ds(unit, unit), pl.ds(2 * unit, unit)
        q2a, q2b = pl.ds(2 * unit, unit // 2), pl.ds(2 * unit + unit // 2, unit // 2)

        def own_send(slot, rows, to):
            c = remote(pts_in.at[core, rows], pts.at[ho, rows], ag_send.at[slot], ag_recv.at[slot], to)
            c.start()
            pending.append(c)
            return c

        def relay(slot, j, rows, to):
            ref = pts.at[j, rows]
            c = remote(ref, ref, ag_send.at[slot], ag_recv.at[slot], to)
            c.start()
            pending.append(c)
            return c

        shared = {}

        def share(name, j, rows):
            c = forward(len(shared), j, rows)
            shared[name] = c
            pending.append(c)

        x_f = own_send(0, first, to_x)
        y_f = own_send(1, first, to_y)
        x_1 = own_send(2, q1, to_x)
        y_2 = own_send(3, q2, to_y)
        y_1 = own_send(4, q1, to_y)
        own_copy.wait()
        many_scores([2 * d, 2 * d + 1])
        y_f.wait_recv()
        x_rf = relay(5, hy, first, to_x)
        x_2b = own_send(6, q2b, to_x)
        x_2a = own_send(7, q2a, to_x)
        z_y = relay(8, hy, first, to_z)
        share("yf", hy, first)
        x_f.wait_recv()
        z_x = relay(9, hx, first, to_z)
        share("xf", hx, first)
        x_1.wait_recv()
        y_r1 = relay(10, hx, q1, to_y)
        share("x1", hx, q1)
        y_2.wait_recv()
        x_r2 = relay(11, hy, q2a, to_x)
        share("y2", hy, q2)
        z_y.wait_recv()
        share("yo", hy, other)
        x_rf.wait_recv()
        z_d = relay(12, hd, first, to_z)
        share("df", hd, first)
        y_1.wait_recv()
        share("y1", hy, q1)
        x_2b.wait_recv()
        y_r2 = relay(13, hx, q2b, to_y)
        many_scores([hy])
        z_x.wait_recv()
        share("xo", hx, other)
        x_2a.wait_recv()
        share("x2", hx, q2)
        for name in ("yf", "y2", "yo", "y1"):
            shared[name].wait_recv()
        many_scores([flip(hy, 1), hx])
        y_r1.wait_recv()
        share("d1", hd, q1)
        for name in ("xf", "x1", "xo", "x2"):
            shared[name].wait_recv()
        many_scores([flip(hx, 1)])
        x_r2.wait_recv()
        share("da", hd, q2a)
        y_r2.wait_recv()
        share("db", hd, q2b)
        z_d.wait_recv()
        share("do", hd, other)
        many_scores([hd])
        for name in ("df", "d1", "da", "db", "do"):
            shared[name].wait_recv()
        many_scores([flip(hd, 1)])
    else:
        sends = []
        for o in range(1, n_dp):
            c = remote(
                pts_in.at[core], pts.at[2 * d + core], ag_send.at[o - 1], ag_recv.at[o - 1],
                {"dp": lax.rem(d + o, n_dp), "cent": k},
            )
            c.start()
            sends.append(c)
        own_copy.wait()
        many_scores([2 * d, 2 * d + 1])
        forwards = []
        for o in range(1, n_dp):
            sends[o - 1].wait_recv()
            j = 2 * lax.rem(d + n_dp - o, n_dp) + core
            forwards.append(forward(o - 1, j, pl.ds(0, blk)))
        for o in range(1, n_dp):
            j = 2 * lax.rem(d + n_dp - o, n_dp) + core
            many_scores([j])
            forwards[o - 1].wait_recv()
            many_scores([flip(j, 1)])
        pending = sends + forwards
    for c in pending:
        c.wait_send()

    def finish_columns():
        for s in strips:
            t = top[s, :]
            m = jnp.max(t, axis=1, keepdims=True)
            total = jnp.sum(tot[s, :] * jnp.exp2(t - m), axis=1, keepdims=True)
            cp[s, :] = jnp.broadcast_to(log_ratio - (m + jnp.log2(total)), (strip, LANES))

    def put_chunks(x, i, v):
        for g in range(per):
            w = i * per + g
            mine[x, w] = v[:, g * LANES : (g + 1) * LANES]
            for group in range(n // w_all):
                owner = group * w_all + w

                @pl.when(owner != me)
                def _():
                    remote(
                        mine.at[x, w], gathered.at[x, me], x1_send.at[x], x1_recv.at[x], dev(owner)
                    ).start()

    def row_pass(ref, x):
        def body(i, _):
            def inner(s):
                return ref[i, s, :] + tile_lanes(cp[s, :], blk)

            m8 = fold(jnp.maximum, [sub8(jnp.maximum, inner(s)) for s in strips])
            rmax = jnp.max(m8, axis=0, keepdims=True)
            part_sum = None
            for s in strips:
                e = jnp.exp2(inner(s) - rmax)
                ref[i, s, :] = e
                t = sub8(jnp.add, e)
                part_sum = t if part_sum is None else part_sum + t
            total = jnp.sum(part_sum, axis=0, keepdims=True)
            row_m[i] = rmax
            put_chunks(x, i, rmax + jnp.log2(total))
            return 0

        lax.fori_loop(0, nb, body, 0)

    def wait_bytes(ref, sem):
        pltpu.make_async_copy(ref, ref, sem).wait()

    def middle_exchange(x, logs):
        wait_bytes(gathered.at[x, pl.ds(0, n - 1)], x1_recv.at[x])
        wait_bytes(gathered.at[x, pl.ds(0, n - 1)], x1_send.at[x])
        gathered[x, me] = mine[x, my_w]
        v = gathered[x]
        if logs:
            m = jnp.max(v, axis=0, keepdims=True)
            res = m + jnp.log2(jnp.sum(jnp.exp2(v - m), axis=0, keepdims=True))
        else:
            res = jnp.sum(v, axis=0, keepdims=True)
        full[x, my_w] = res[0]

        def send(o, _):
            e = (me // w_all) * w_all + lax.rem(my_w + o, w_all)
            ref = full.at[x, my_w]
            remote(ref, ref, x2_send.at[x], x2_recv.at[2 * x + my_half], dev(e)).start()
            return 0

        lax.fori_loop(1, w_all, send, 0)

    def end_exchange(x, half):
        @pl.when(my_half == half)
        def _():
            wait_bytes(full.at[x, pl.ds(0, w_half - 1)], x2_recv.at[2 * x + half])

        @pl.when(my_half != half)
        def _():
            wait_bytes(full.at[x, pl.ds(0, w_half)], x2_recv.at[2 * x + half])

        if half:
            wait_bytes(full.at[x, pl.ds(0, w_all - 1)], x2_send.at[x])

    def full_row(x, i):
        return jnp.concatenate([full[x, i * per + g] for g in range(per)], axis=1)

    def weigh(ref, scale_of, x=None):
        mass[...] = jnp.zeros_like(mass)
        acc[...] = jnp.zeros_like(acc)

        def body(i, _):
            scale = scale_of(i)
            for s in strips:
                p = ref[i, s, :] * scale
                mass[s, :] += fold(jnp.add, lane_groups(p))
                pb[s, :] = p.astype(jnp.bfloat16)
            acc[...] += jnp.dot(pb[...], pts[i], preferred_element_type=jnp.float32)
            return 0

        for h in range(2):
            if x is not None:
                end_exchange(x, h)
            lax.fori_loop(h * nb // 2, (h + 1) * nb // 2, body, 0)

    def refresh(out, used, gain):
        for s in strips:
            m = jnp.sum(mass[s, :], axis=1, keepdims=True)
            wgt = acc[s, :]
            if gain:
                r = ratio_j[s, :][:, 0:1]
                m, wgt = m * r, wgt * r
            fresh = (wgt + prior * used[s, :].astype(jnp.float32)) / (m + prior)
            out[s, :] = fresh.astype(jnp.bfloat16)

    finish_columns()
    row_pass(lt, 0)
    middle_exchange(0, True)

    def scale_0(i):
        v = jnp.exp2(row_m[i] - full_row(0, i))
        row_a[i] = v
        return v

    weigh(lt, scale_0, 0)
    refresh(c1, cen, False)
    for s in strips:
        m = jnp.sum(mass[s, :], axis=1, keepdims=True)
        ratio_j[s, :] = jnp.broadcast_to(2.0**log_ratio / m, (strip, LANES))

    def row_sums(i, _):
        part_sum = fold(
            jnp.add,
            [sub8(jnp.add, lt[i, s, :] * tile_lanes(ratio_j[s, :], blk)) for s in strips],
        )
        put_chunks(1, i, jnp.sum(part_sum, axis=0, keepdims=True) * row_a[i])
        return 0

    lax.fori_loop(0, nb, row_sums, 0)

    def second_scores(i, _):
        dot_scores(c1, i, lt2)
        return 0

    lax.fori_loop(0, nb // 2, second_scores, 0)
    middle_exchange(1, False)
    lax.fori_loop(nb // 2, nb, second_scores, 0)

    top[...] = jnp.full_like(top, -jnp.inf)
    tot[...] = jnp.zeros_like(tot)

    def second_columns(i, _):
        t = full_row(1, i)
        row_b[i] = row_a[i] / t
        pot = -full_row(0, i) - jnp.log2(t)
        for s in strips:
            online(lt2[i, s, :] + pot, s)
        return 0

    for h in range(2):
        end_exchange(1, h)
        lax.fori_loop(h * nb // 2, (h + 1) * nb // 2, second_columns, 0)
    finish_columns()
    row_pass(lt2, 2)
    middle_exchange(2, True)
    weigh(lt, lambda i: row_b[i])
    refresh(previous, cen, True)
    weigh(lt2, lambda i: jnp.exp2(row_m[i] - full_row(2, i)), 2)
    refresh(newest, c1, False)
    for h in range(2):
        row_out[h] = -LN2 * full_row(2, 2 * d + h)
    list_out[...] = LN2 * cp[...].T[0:1, :]


def shards(n_dp, n_cent, points, centroids):
    rows, width = points.shape
    lists = centroids.shape[0]
    n = n_dp * n_cent
    blk = rows // 2
    nb = 2 * n_dp
    w_all = rows * n_dp // LANES
    f32, bf16 = jnp.float32, jnp.bfloat16
    dma = pltpu.SemaphoreType.DMA
    vmem = pl.BlockSpec(memory_space=pltpu.VMEM)
    newest, previous, row_pot, list_pot = pl.pallas_call(
        functools.partial(kernel, n_dp, n_cent),
        out_shape=(
            jax.ShapeDtypeStruct((lists, width), bf16),
            jax.ShapeDtypeStruct((lists, width), bf16),
            jax.ShapeDtypeStruct((2, 1, blk), f32),
            jax.ShapeDtypeStruct((1, lists), f32),
        ),
        in_specs=[pl.BlockSpec(memory_space=pl.ANY), vmem],
        out_specs=(vmem, vmem, vmem, vmem),
        scratch_shapes=[
            pltpu.VMEM((nb, blk, width), bf16),
            pltpu.VMEM((nb, lists, blk), f32),
            pltpu.VMEM((nb, lists, blk), f32),
            pltpu.VMEM((lists, blk), bf16),
            pltpu.VMEM((lists, width), f32),
            pltpu.VMEM((lists, width), bf16),
            pltpu.VMEM((lists, LANES), f32),
            pltpu.VMEM((lists, LANES), f32),
            pltpu.VMEM((lists, LANES), f32),
            pltpu.VMEM((lists, LANES), f32),
            pltpu.VMEM((lists, LANES), f32),
            pltpu.VMEM((nb, 1, blk), f32),
            pltpu.VMEM((nb, 1, blk), f32),
            pltpu.VMEM((nb, 1, blk), f32),
            pltpu.VMEM((3, w_all, 1, LANES), f32),
            pltpu.VMEM((3, n, 1, LANES), f32),
            pltpu.VMEM((3, w_all, 1, LANES), f32),
            dma, dma((14,)), dma((14,)), dma((13,)), dma((13,)),
            dma((3,)), dma((3,)), dma((3,)), dma((6,)),
        ],
        compiler_params=pltpu.CompilerParams(
            collective_id=0, has_side_effects=True, vmem_limit_bytes=52 * 1024 * 1024
        ),
    )(points.reshape(2, blk, width), centroids)
    return newest, previous, row_pot.reshape(rows), list_pot.reshape(lists)


def solution(mesh):
    return jax.shard_map(
        functools.partial(shards, mesh.shape["dp"], mesh.shape["cent"]),
        mesh=mesh,
        in_specs=(P("dp", None), P(("cent", "dp"), None)),
        out_specs=(P(("cent", "dp"), None), P(("cent", "dp"), None), P("dp"), P(("cent", "dp"))),
        check_vma=False,
    )
```

```python
import functools
import math

import jax
import jax.numpy as jnp
from jax import lax
from jax.experimental import pallas as pl
from jax.experimental.pallas import tpu as pltpu
from jax.sharding import PartitionSpec as P

sharpness = 4.0
LANES = 128
LOG2E = math.log2(math.e)
LN2 = math.log(2.0)


def flip(i, bit):
    return i + bit - 2 * bit * ((i // bit) % 2)


def tile_lanes(col, width):
    return jnp.concatenate([col] * (width // LANES), axis=1)


def lane_groups(x):
    return [x[:, g : g + LANES] for g in range(0, x.shape[1], LANES)]


def fold(op, parts):
    return functools.reduce(op, parts)


def sub8(op, x):
    return fold(op, [x[g : g + 8] for g in range(0, x.shape[0], 8)])


def kernel(
    n_dp, n_cent,
    pts_in, cen,
    newest, previous, row_out, list_out,
    pts, lt, lt2, pb, pb2, acc, c1, top, tot, cp, ratio_j, mass, row_a, row_b, row_m,
    mine, gathered, full,
    own_sem, ag_send, ag_recv, sib_send, sib_recv, x1_send, x1_recv, x2_send, x2_recv,
):
    n = n_dp * n_cent
    _, blk, width = pts_in.shape
    nb = 2 * n_dp
    lists = cen.shape[0]
    rows_all = nb * blk
    w_all = rows_all // LANES
    per = blk // LANES
    quarter = blk // 2
    log_ratio = math.log2(rows_all / (lists * n))
    prior = 0.5 * rows_all / (lists * n)
    factor = sharpness / math.sqrt(width) * LOG2E
    strip = 64
    strips = [pl.ds(s, strip) for s in range(0, lists, strip)]

    d = lax.axis_index("dp")
    k = lax.axis_index("cent")
    core = lax.rem(k, 2)
    sib = flip(k, 1)
    me = k * n_dp + d
    my_w = lax.rem(me, w_all)
    w_half = w_all // 2
    my_half = my_w // w_half

    def dev(e):
        return {"dp": lax.rem(e, n_dp), "cent": e // n_dp}

    barrier = pltpu.get_barrier_semaphore()

    def greet(o, _):
        e = lax.rem(me + o, n)
        pl.semaphore_signal(barrier, inc=1, device_id=dev(e), device_id_type=pl.DeviceIdType.MESH)
        return 0

    lax.fori_loop(1, n, greet, 0)
    own_copy = pltpu.make_async_copy(pts_in, pts.at[pl.ds(2 * d, 2)], own_sem)
    own_copy.start()
    top[...] = jnp.full_like(top, -jnp.inf)
    tot[...] = jnp.zeros_like(tot)
    pl.semaphore_wait(barrier, n - 1)

    def remote(src, dst, ss, rs, to):
        return pltpu.make_async_remote_copy(
            src_ref=src, dst_ref=dst, send_sem=ss, recv_sem=rs,
            device_id=to, device_id_type=pl.DeviceIdType.MESH,
        )

    def online(x, s):
        groups = lane_groups(x)
        old = top[s, :]
        new = jnp.maximum(old, fold(jnp.maximum, groups))
        tot[s, :] = tot[s, :] * jnp.exp2(old - new) + fold(
            jnp.add, [jnp.exp2(g - new) for g in groups]
        )
        top[s, :] = new

    def dot_scores(c_ref, i, out):
        for q in range(2):
            lanes = pl.ds(q * quarter, quarter)
            out[i, :, lanes] = factor * lax.dot_general(
                c_ref[...], pts[i, lanes, :], (((1,), (1,)), ((), ())),
                preferred_element_type=jnp.float32,
            )

    def first_scores(i):
        dot_scores(cen, i, lt)
        for s in strips:
            online(lt[i, s, :], s)

    def many_scores(blocks):
        def body(t, _):
            i = blocks[0]
            for u in range(1, len(blocks)):
                i = jnp.where(t == u, blocks[u], i)
            first_scores(i)
            return 0

        lax.fori_loop(0, len(blocks), body, 0)

    def forward(slot, j, rows):
        ref = pts.at[j, rows]
        cp_ = remote(ref, ref, sib_send.at[slot], sib_recv.at[slot], {"dp": d, "cent": sib})
        cp_.start()
        return cp_

    pending = []
    if n_dp == 4 and n_cent % 4 == 0:
        dx, dy = flip(d, 1), flip(d, 2)
        dd = flip(dx, 2)
        hx, hy, hd, ho = 2 * dx + core, 2 * dy + core, 2 * dd + core, 2 * d + core
        to_x, to_y = {"dp": dx, "cent": k}, {"dp": dy, "cent": k}
        to_z = {"dp": d, "cent": flip(k, 2)}
        unit = blk // 4
        odd = lax.rem(k // 2, 2)
        first = pl.ds(pl.multiple_of(odd * 3 * unit, unit), unit)
        other = pl.ds(pl.multiple_of((1 - odd) * 3 * unit, unit), unit)
        q1, q2 = pl.ds(unit, unit), pl.ds(2 * unit, unit)
        q2a, q2b = pl.ds(2 * unit, unit // 2), pl.ds(2 * unit + unit // 2, unit // 2)

        def own_send(slot, rows, to):
            c = remote(pts_in.at[core, rows], pts.at[ho, rows], ag_send.at[slot], ag_recv.at[slot], to)
            c.start()
            pending.append(c)
            return c

        def relay(slot, j, rows, to):
            ref = pts.at[j, rows]
            c = remote(ref, ref, ag_send.at[slot], ag_recv.at[slot], to)
            c.start()
            pending.append(c)
            return c

        shared = {}

        def share(name, j, rows):
            c = forward(len(shared), j, rows)
            shared[name] = c
            pending.append(c)

        x_f = own_send(0, first, to_x)
        y_f = own_send(1, first, to_y)
        x_1 = own_send(2, q1, to_x)
        y_2 = own_send(3, q2, to_y)
        y_1 = own_send(4, q1, to_y)
        own_copy.wait()
        many_scores([2 * d, 2 * d + 1])
        y_f.wait_recv()
        x_rf = relay(5, hy, first, to_x)
        x_2b = own_send(6, q2b, to_x)
        x_2a = own_send(7, q2a, to_x)
        z_y = relay(8, hy, first, to_z)
        share("yf", hy, first)
        x_f.wait_recv()
        z_x = relay(9, hx, first, to_z)
        share("xf", hx, first)
        x_1.wait_recv()
        y_r1 = relay(10, hx, q1, to_y)
        share("x1", hx, q1)
        y_2.wait_recv()
        x_r2 = relay(11, hy, q2a, to_x)
        share("y2", hy, q2)
        z_y.wait_recv()
        share("yo", hy, other)
        x_rf.wait_recv()
        z_d = relay(12, hd, first, to_z)
        share("df", hd, first)
        y_1.wait_recv()
        share("y1", hy, q1)
        x_2b.wait_recv()
        y_r2 = relay(13, hx, q2b, to_y)
        many_scores([hy])
        z_x.wait_recv()
        share("xo", hx, other)
        x_2a.wait_recv()
        share("x2", hx, q2)
        for name in ("yf", "y2", "yo", "y1"):
            shared[name].wait_recv()
        many_scores([flip(hy, 1), hx])
        y_r1.wait_recv()
        share("d1", hd, q1)
        for name in ("xf", "x1", "xo", "x2"):
            shared[name].wait_recv()
        many_scores([flip(hx, 1)])
        x_r2.wait_recv()
        share("da", hd, q2a)
        y_r2.wait_recv()
        share("db", hd, q2b)
        z_d.wait_recv()
        share("do", hd, other)
        many_scores([hd])
        for name in ("df", "d1", "da", "db", "do"):
            shared[name].wait_recv()
        many_scores([flip(hd, 1)])
    else:
        sends = []
        for o in range(1, n_dp):
            c = remote(
                pts_in.at[core], pts.at[2 * d + core], ag_send.at[o - 1], ag_recv.at[o - 1],
                {"dp": lax.rem(d + o, n_dp), "cent": k},
            )
            c.start()
            sends.append(c)
        own_copy.wait()
        many_scores([2 * d, 2 * d + 1])
        forwards = []
        for o in range(1, n_dp):
            sends[o - 1].wait_recv()
            j = 2 * lax.rem(d + n_dp - o, n_dp) + core
            forwards.append(forward(o - 1, j, pl.ds(0, blk)))
        for o in range(1, n_dp):
            j = 2 * lax.rem(d + n_dp - o, n_dp) + core
            many_scores([j])
            forwards[o - 1].wait_recv()
            many_scores([flip(j, 1)])
        pending = sends + forwards
    for c in pending:
        c.wait_send()

    def finish_columns():
        for s in strips:
            t = top[s, :]
            m = jnp.max(t, axis=1, keepdims=True)
            total = jnp.sum(tot[s, :] * jnp.exp2(t - m), axis=1, keepdims=True)
            cp[s, :] = jnp.broadcast_to(log_ratio - (m + jnp.log2(total)), (strip, LANES))

    def put_chunks(x, i, v):
        for g in range(per):
            w = i * per + g
            mine[x, w] = v[:, g * LANES : (g + 1) * LANES]
            for group in range(n // w_all):
                owner = group * w_all + w

                @pl.when(owner != me)
                def _():
                    remote(
                        mine.at[x, w], gathered.at[x, me], x1_send.at[x], x1_recv.at[x], dev(owner)
                    ).start()

    def row_pass(ref, x):
        def body(i, _):
            def inner(s):
                return ref[i, s, :] + tile_lanes(cp[s, :], blk)

            m8 = fold(jnp.maximum, [sub8(jnp.maximum, inner(s)) for s in strips])
            rmax = jnp.max(m8, axis=0, keepdims=True)
            part_sum = None
            for s in strips:
                e = jnp.exp2(inner(s) - rmax)
                ref[i, s, :] = e
                t = sub8(jnp.add, e)
                part_sum = t if part_sum is None else part_sum + t
            total = jnp.sum(part_sum, axis=0, keepdims=True)
            row_m[i] = rmax
            put_chunks(x, i, rmax + jnp.log2(total))
            return 0

        lax.fori_loop(0, nb, body, 0)

    def wait_bytes(ref, sem):
        pltpu.make_async_copy(ref, ref, sem).wait()

    def middle_exchange(x, logs):
        wait_bytes(gathered.at[x, pl.ds(0, n - 1)], x1_recv.at[x])
        wait_bytes(gathered.at[x, pl.ds(0, n - 1)], x1_send.at[x])
        gathered[x, me] = mine[x, my_w]
        v = gathered[x]
        if logs:
            m = jnp.max(v, axis=0, keepdims=True)
            res = m + jnp.log2(jnp.sum(jnp.exp2(v - m), axis=0, keepdims=True))
        else:
            res = jnp.sum(v, axis=0, keepdims=True)
        full[x, my_w] = res[0]

        def send(o, _):
            e = (me // w_all) * w_all + lax.rem(my_w + o, w_all)
            ref = full.at[x, my_w]
            remote(ref, ref, x2_send.at[x], x2_recv.at[2 * x + my_half], dev(e)).start()
            return 0

        lax.fori_loop(1, w_all, send, 0)

    def end_exchange(x, half):
        @pl.when(my_half == half)
        def _():
            wait_bytes(full.at[x, pl.ds(0, w_half - 1)], x2_recv.at[2 * x + half])

        @pl.when(my_half != half)
        def _():
            wait_bytes(full.at[x, pl.ds(0, w_half)], x2_recv.at[2 * x + half])

        if half:
            wait_bytes(full.at[x, pl.ds(0, w_all - 1)], x2_send.at[x])

    def full_row(x, i):
        return jnp.concatenate([full[x, i * per + g] for g in range(per)], axis=1)

    def weigh(ref, scale_of, x=None):
        mass[...] = jnp.zeros_like(mass)
        acc[...] = jnp.zeros_like(acc)

        def fill(to, i):
            scale = scale_of(i)
            for s in strips:
                p = ref[i, s, :] * scale
                mass[s, :] += fold(jnp.add, lane_groups(p))
                to[s, :] = p.astype(jnp.bfloat16)

        slots = (pb, pb2)
        steps = 4
        groups = nb // steps

        def body(t, _):
            if x is not None:
                for h in range(2):

                    @pl.when(t == h * (groups // 2))
                    def _():
                        end_exchange(x, h)

            fill(slots[0], t * steps)
            for u in range(steps):
                if u + 1 < steps:
                    fill(slots[(u + 1) % 2], t * steps + u + 1)
                acc[...] += jnp.dot(
                    slots[u % 2][...], pts[t * steps + u], preferred_element_type=jnp.float32
                )
            return 0

        lax.fori_loop(0, groups, body, 0)

    def refresh(out, used, gain):
        for s in strips:
            m = jnp.sum(mass[s, :], axis=1, keepdims=True)
            wgt = acc[s, :]
            if gain:
                r = ratio_j[s, :][:, 0:1]
                m, wgt = m * r, wgt * r
            fresh = (wgt + prior * used[s, :].astype(jnp.float32)) / (m + prior)
            out[s, :] = fresh.astype(jnp.bfloat16)

    finish_columns()
    row_pass(lt, 0)
    middle_exchange(0, True)

    def scale_0(i):
        v = jnp.exp2(row_m[i] - full_row(0, i))
        row_a[i] = v
        return v

    weigh(lt, scale_0, 0)
    refresh(c1, cen, False)
    for s in strips:
        m = jnp.sum(mass[s, :], axis=1, keepdims=True)
        ratio_j[s, :] = jnp.broadcast_to(2.0**log_ratio / m, (strip, LANES))

    def row_sums(i, _):
        part_sum = fold(
            jnp.add,
            [sub8(jnp.add, lt[i, s, :] * tile_lanes(ratio_j[s, :], blk)) for s in strips],
        )
        put_chunks(1, i, jnp.sum(part_sum, axis=0, keepdims=True) * row_a[i])
        return 0

    lax.fori_loop(0, nb, row_sums, 0)

    def second_scores(i, _):
        dot_scores(c1, i, lt2)
        return 0

    lax.fori_loop(0, nb // 2, second_scores, 0)
    middle_exchange(1, False)
    lax.fori_loop(nb // 2, nb, second_scores, 0)

    top[...] = jnp.full_like(top, -jnp.inf)
    tot[...] = jnp.zeros_like(tot)

    def second_columns(i, _):
        t = full_row(1, i)
        row_b[i] = row_a[i] / t
        pot = -full_row(0, i) - jnp.log2(t)
        for s in strips:
            online(lt2[i, s, :] + pot, s)
        return 0

    for h in range(2):
        end_exchange(1, h)
        lax.fori_loop(h * nb // 2, (h + 1) * nb // 2, second_columns, 0)
    finish_columns()
    row_pass(lt2, 2)
    middle_exchange(2, True)
    weigh(lt, lambda i: row_b[i])
    refresh(previous, cen, True)
    weigh(lt2, lambda i: jnp.exp2(row_m[i] - full_row(2, i)), 2)
    refresh(newest, c1, False)
    for h in range(2):
        row_out[h] = -LN2 * full_row(2, 2 * d + h)
    list_out[...] = LN2 * cp[...].T[0:1, :]


def shards(n_dp, n_cent, points, centroids):
    rows, width = points.shape
    lists = centroids.shape[0]
    n = n_dp * n_cent
    blk = rows // 2
    nb = 2 * n_dp
    w_all = rows * n_dp // LANES
    f32, bf16 = jnp.float32, jnp.bfloat16
    dma = pltpu.SemaphoreType.DMA
    vmem = pl.BlockSpec(memory_space=pltpu.VMEM)
    newest, previous, row_pot, list_pot = pl.pallas_call(
        functools.partial(kernel, n_dp, n_cent),
        out_shape=(
            jax.ShapeDtypeStruct((lists, width), bf16),
            jax.ShapeDtypeStruct((lists, width), bf16),
            jax.ShapeDtypeStruct((2, 1, blk), f32),
            jax.ShapeDtypeStruct((1, lists), f32),
        ),
        in_specs=[pl.BlockSpec(memory_space=pl.ANY), vmem],
        out_specs=(vmem, vmem, vmem, vmem),
        scratch_shapes=[
            pltpu.VMEM((nb, blk, width), bf16),
            pltpu.VMEM((nb, lists, blk), f32),
            pltpu.VMEM((nb, lists, blk), f32),
            pltpu.VMEM((lists, blk), bf16),
            pltpu.VMEM((lists, blk), bf16),
            pltpu.VMEM((lists, width), f32),
            pltpu.VMEM((lists, width), bf16),
            pltpu.VMEM((lists, LANES), f32),
            pltpu.VMEM((lists, LANES), f32),
            pltpu.VMEM((lists, LANES), f32),
            pltpu.VMEM((lists, LANES), f32),
            pltpu.VMEM((lists, LANES), f32),
            pltpu.VMEM((nb, 1, blk), f32),
            pltpu.VMEM((nb, 1, blk), f32),
            pltpu.VMEM((nb, 1, blk), f32),
            pltpu.VMEM((3, w_all, 1, LANES), f32),
            pltpu.VMEM((3, n, 1, LANES), f32),
            pltpu.VMEM((3, w_all, 1, LANES), f32),
            dma, dma((14,)), dma((14,)), dma((13,)), dma((13,)),
            dma((3,)), dma((3,)), dma((3,)), dma((6,)),
        ],
        compiler_params=pltpu.CompilerParams(
            collective_id=0, has_side_effects=True, vmem_limit_bytes=52 * 1024 * 1024
        ),
    )(points.reshape(2, blk, width), centroids)
    return newest, previous, row_pot.reshape(rows), list_pot.reshape(lists)


def solution(mesh):
    return jax.shard_map(
        functools.partial(shards, mesh.shape["dp"], mesh.shape["cent"]),
        mesh=mesh,
        in_specs=(P("dp", None), P(("cent", "dp"), None)),
        out_specs=(P(("cent", "dp"), None), P(("cent", "dp"), None), P("dp"), P(("cent", "dp"))),
        check_vma=False,
    )
```

```python
import functools
import math

import jax
import jax.numpy as jnp
from jax import lax
from jax.experimental import pallas as pl
from jax.experimental.pallas import tpu as pltpu
from jax.sharding import PartitionSpec as P

sharpness = 4.0
LANES = 128
LOG2E = math.log2(math.e)
LN2 = math.log(2.0)


def flip(i, bit):
    return i + bit - 2 * bit * ((i // bit) % 2)


def tile_lanes(col, width):
    return jnp.concatenate([col] * (width // LANES), axis=1)


def lane_groups(x):
    return [x[:, g : g + LANES] for g in range(0, x.shape[1], LANES)]


def fold(op, parts):
    return functools.reduce(op, parts)


def sub8(op, x):
    return fold(op, [x[g : g + 8] for g in range(0, x.shape[0], 8)])


def kernel(
    n_dp, n_cent,
    pts_in, cen,
    newest, previous, row_out, list_out,
    pts, lt, lt2, pb, pb2, acc, c1, top, tot, cp, ratio_j, mass, row_a, row_b, row_m,
    mine, gathered, full,
    own_sem, rounds, ag_send, ag_recv, sib_send, sib_recv, x1_send, x1_recv, x2_send, x2_recv,
):
    n = n_dp * n_cent
    _, blk, width = pts_in.shape
    nb = 2 * n_dp
    lists = cen.shape[0]
    rows_all = nb * blk
    w_all = rows_all // LANES
    per = blk // LANES
    quarter = blk // 2
    log_ratio = math.log2(rows_all / (lists * n))
    prior = 0.5 * rows_all / (lists * n)
    factor = sharpness / math.sqrt(width) * LOG2E
    strip = 64
    strips = [pl.ds(s, strip) for s in range(0, lists, strip)]

    d = lax.axis_index("dp")
    k = lax.axis_index("cent")
    core = lax.rem(k, 2)
    sib = flip(k, 1)
    me = k * n_dp + d
    my_w = lax.rem(me, w_all)
    w_half = w_all // 2
    my_half = my_w // w_half

    def dev(e):
        return {"dp": lax.rem(e, n_dp), "cent": e // n_dp}

    barrier = pltpu.get_barrier_semaphore()

    partners = [{"dp": flip(d, 1 << b), "cent": k} for b in range(n_dp.bit_length() - 1)]
    partners += [{"dp": d, "cent": flip(k, 1 << b)} for b in range(n_cent.bit_length() - 1)]
    for to in partners:
        pl.semaphore_signal(barrier, inc=1, device_id=to, device_id_type=pl.DeviceIdType.MESH)
    own_copy = pltpu.make_async_copy(pts_in, pts.at[pl.ds(2 * d, 2)], own_sem)
    own_copy.start()
    top[...] = jnp.full_like(top, -jnp.inf)
    tot[...] = jnp.zeros_like(tot)
    pl.semaphore_wait(barrier, len(partners))

    def tell(r):
        pl.semaphore_signal(
            rounds.at[r], inc=1, device_id=partners[r], device_id_type=pl.DeviceIdType.MESH
        )

    def hear(r):
        pl.semaphore_wait(rounds.at[r], 1)

    def remote(src, dst, ss, rs, to):
        return pltpu.make_async_remote_copy(
            src_ref=src, dst_ref=dst, send_sem=ss, recv_sem=rs,
            device_id=to, device_id_type=pl.DeviceIdType.MESH,
        )

    def online(x, s):
        groups = lane_groups(x)
        old = top[s, :]
        new = jnp.maximum(old, fold(jnp.maximum, groups))
        tot[s, :] = tot[s, :] * jnp.exp2(old - new) + fold(
            jnp.add, [jnp.exp2(g - new) for g in groups]
        )
        top[s, :] = new

    def dot_scores(c_ref, i, out):
        for q in range(2):
            lanes = pl.ds(q * quarter, quarter)
            out[i, :, lanes] = factor * lax.dot_general(
                c_ref[...], pts[i, lanes, :], (((1,), (1,)), ((), ())),
                preferred_element_type=jnp.float32,
            )

    def first_scores(i):
        dot_scores(cen, i, lt)
        for s in strips:
            online(lt[i, s, :], s)

    def many_scores(blocks):
        def body(t, _):
            i = blocks[0]
            for u in range(1, len(blocks)):
                i = jnp.where(t == u, blocks[u], i)
            first_scores(i)
            return 0

        lax.fori_loop(0, len(blocks), body, 0)

    def forward(slot, j, rows):
        ref = pts.at[j, rows]
        cp_ = remote(ref, ref, sib_send.at[slot], sib_recv.at[slot], {"dp": d, "cent": sib})
        cp_.start()
        return cp_

    pending = []
    if n_dp == 4 and n_cent == 8:
        dx, dy = flip(d, 1), flip(d, 2)
        dd = flip(dx, 2)
        hx, hy, hd, ho = 2 * dx + core, 2 * dy + core, 2 * dd + core, 2 * d + core
        to_x, to_y = {"dp": dx, "cent": k}, {"dp": dy, "cent": k}
        to_z = {"dp": d, "cent": flip(k, 2)}
        unit = blk // 4
        odd = lax.rem(k // 2, 2)
        first = pl.ds(pl.multiple_of(odd * 3 * unit, unit), unit)
        other = pl.ds(pl.multiple_of((1 - odd) * 3 * unit, unit), unit)
        q1, q2 = pl.ds(unit, unit), pl.ds(2 * unit, unit)
        q2a, q2b = pl.ds(2 * unit, unit // 2), pl.ds(2 * unit + unit // 2, unit // 2)

        def own_send(slot, rows, to):
            c = remote(pts_in.at[core, rows], pts.at[ho, rows], ag_send.at[slot], ag_recv.at[slot], to)
            c.start()
            pending.append(c)
            return c

        def relay(slot, j, rows, to):
            ref = pts.at[j, rows]
            c = remote(ref, ref, ag_send.at[slot], ag_recv.at[slot], to)
            c.start()
            pending.append(c)
            return c

        shared = {}

        def share(name, j, rows):
            c = forward(len(shared), j, rows)
            shared[name] = c
            pending.append(c)

        x_f = own_send(0, first, to_x)
        y_f = own_send(1, first, to_y)
        x_1 = own_send(2, q1, to_x)
        y_2 = own_send(3, q2, to_y)
        y_1 = own_send(4, q1, to_y)
        tell(0)
        own_copy.wait()
        many_scores([2 * d, 2 * d + 1])
        hear(0)
        tell(1)
        y_f.wait_recv()
        x_rf = relay(5, hy, first, to_x)
        x_2b = own_send(6, q2b, to_x)
        x_2a = own_send(7, q2a, to_x)
        z_y = relay(8, hy, first, to_z)
        share("yf", hy, first)
        x_f.wait_recv()
        z_x = relay(9, hx, first, to_z)
        share("xf", hx, first)
        hear(1)
        tell(2)
        x_1.wait_recv()
        y_r1 = relay(10, hx, q1, to_y)
        share("x1", hx, q1)
        y_2.wait_recv()
        x_r2 = relay(11, hy, q2a, to_x)
        share("y2", hy, q2)
        hear(2)
        tell(3)
        z_y.wait_recv()
        share("yo", hy, other)
        x_rf.wait_recv()
        z_d = relay(12, hd, first, to_z)
        share("df", hd, first)
        y_1.wait_recv()
        share("y1", hy, q1)
        hear(3)
        tell(4)
        x_2b.wait_recv()
        y_r2 = relay(13, hx, q2b, to_y)
        many_scores([hy])
        hear(4)
        z_x.wait_recv()
        share("xo", hx, other)
        x_2a.wait_recv()
        share("x2", hx, q2)
        for name in ("yf", "y2", "yo", "y1"):
            shared[name].wait_recv()
        many_scores([flip(hy, 1), hx])
        y_r1.wait_recv()
        share("d1", hd, q1)
        for name in ("xf", "x1", "xo", "x2"):
            shared[name].wait_recv()
        many_scores([flip(hx, 1)])
        x_r2.wait_recv()
        share("da", hd, q2a)
        y_r2.wait_recv()
        share("db", hd, q2b)
        z_d.wait_recv()
        share("do", hd, other)
        many_scores([hd])
        for name in ("df", "d1", "da", "db", "do"):
            shared[name].wait_recv()
        many_scores([flip(hd, 1)])
    else:
        for r in range(len(partners)):
            tell(r)
            hear(r)
        sends = []
        for o in range(1, n_dp):
            c = remote(
                pts_in.at[core], pts.at[2 * d + core], ag_send.at[o - 1], ag_recv.at[o - 1],
                {"dp": lax.rem(d + o, n_dp), "cent": k},
            )
            c.start()
            sends.append(c)
        own_copy.wait()
        many_scores([2 * d, 2 * d + 1])
        forwards = []
        for o in range(1, n_dp):
            sends[o - 1].wait_recv()
            j = 2 * lax.rem(d + n_dp - o, n_dp) + core
            forwards.append(forward(o - 1, j, pl.ds(0, blk)))
        for o in range(1, n_dp):
            j = 2 * lax.rem(d + n_dp - o, n_dp) + core
            many_scores([j])
            forwards[o - 1].wait_recv()
            many_scores([flip(j, 1)])
        pending = sends + forwards
    for c in pending:
        c.wait_send()

    def finish_columns():
        for s in strips:
            t = top[s, :]
            m = jnp.max(t, axis=1, keepdims=True)
            total = jnp.sum(tot[s, :] * jnp.exp2(t - m), axis=1, keepdims=True)
            cp[s, :] = jnp.broadcast_to(log_ratio - (m + jnp.log2(total)), (strip, LANES))

    def put_chunks(x, i, v):
        for g in range(per):
            w = i * per + g
            mine[x, w] = v[:, g * LANES : (g + 1) * LANES]
            for group in range(n // w_all):
                owner = group * w_all + w

                @pl.when(owner != me)
                def _():
                    remote(
                        mine.at[x, w], gathered.at[x, me], x1_send.at[x], x1_recv.at[x], dev(owner)
                    ).start()

    def row_pass(ref, x):
        def body(i, _):
            def inner(s):
                return ref[i, s, :] + tile_lanes(cp[s, :], blk)

            m8 = fold(jnp.maximum, [sub8(jnp.maximum, inner(s)) for s in strips])
            rmax = jnp.max(m8, axis=0, keepdims=True)
            part_sum = None
            for s in strips:
                e = jnp.exp2(inner(s) - rmax)
                ref[i, s, :] = e
                t = sub8(jnp.add, e)
                part_sum = t if part_sum is None else part_sum + t
            total = jnp.sum(part_sum, axis=0, keepdims=True)
            row_m[i] = rmax
            put_chunks(x, i, rmax + jnp.log2(total))
            return 0

        lax.fori_loop(0, nb, body, 0)

    def wait_bytes(ref, sem):
        pltpu.make_async_copy(ref, ref, sem).wait()

    def middle_exchange(x, logs):
        wait_bytes(gathered.at[x, pl.ds(0, n - 1)], x1_recv.at[x])
        wait_bytes(gathered.at[x, pl.ds(0, n - 1)], x1_send.at[x])
        gathered[x, me] = mine[x, my_w]
        v = gathered[x]
        if logs:
            m = jnp.max(v, axis=0, keepdims=True)
            res = m + jnp.log2(jnp.sum(jnp.exp2(v - m), axis=0, keepdims=True))
        else:
            res = jnp.sum(v, axis=0, keepdims=True)
        full[x, my_w] = res[0]

        ref = full.at[x, my_w]

        def send_to(to):
            remote(ref, ref, x2_send.at[x], x2_recv.at[2 * x + my_half], to).start()

        if n == w_all:
            cents = [lax.rem(k + o, n_cent) for o in range(n_cent)]
            dps = [lax.rem(d + o, n_dp) for o in range(n_dp)]
            for oc in sorted(range(n_cent), key=lambda o: abs(2 * o - n_cent)):
                for od in range(n_dp):
                    if oc or od:
                        send_to({"dp": dps[od], "cent": cents[oc]})
        else:

            def send(o, _):
                send_to(dev((me // w_all) * w_all + lax.rem(my_w + o, w_all)))
                return 0

            lax.fori_loop(1, w_all, send, 0)

    def end_exchange(x, half):
        @pl.when(my_half == half)
        def _():
            wait_bytes(full.at[x, pl.ds(0, w_half - 1)], x2_recv.at[2 * x + half])

        @pl.when(my_half != half)
        def _():
            wait_bytes(full.at[x, pl.ds(0, w_half)], x2_recv.at[2 * x + half])

        if half:
            wait_bytes(full.at[x, pl.ds(0, w_all - 1)], x2_send.at[x])

    def full_row(x, i):
        return jnp.concatenate([full[x, i * per + g] for g in range(per)], axis=1)

    def weigh(ref, scale_of, x=None):
        mass[...] = jnp.zeros_like(mass)
        acc[...] = jnp.zeros_like(acc)

        def fill(to, i):
            scale = scale_of(i)
            for s in strips:
                p = ref[i, s, :] * scale
                mass[s, :] += fold(jnp.add, lane_groups(p))
                to[s, :] = p.astype(jnp.bfloat16)

        slots = (pb, pb2)
        steps = 4
        groups = nb // steps

        def body(t, _):
            if x is not None:
                for h in range(2):

                    @pl.when(t == h * (groups // 2))
                    def _():
                        end_exchange(x, h)

            fill(slots[0], t * steps)
            for u in range(steps):
                if u + 1 < steps:
                    fill(slots[(u + 1) % 2], t * steps + u + 1)
                acc[...] += jnp.dot(
                    slots[u % 2][...], pts[t * steps + u], preferred_element_type=jnp.float32
                )
            return 0

        lax.fori_loop(0, groups, body, 0)

    def refresh(out, used, gain):
        for s in strips:
            m = jnp.sum(mass[s, :], axis=1, keepdims=True)
            wgt = acc[s, :]
            if gain:
                r = ratio_j[s, :][:, 0:1]
                m, wgt = m * r, wgt * r
            fresh = (wgt + prior * used[s, :].astype(jnp.float32)) / (m + prior)
            out[s, :] = fresh.astype(jnp.bfloat16)

    finish_columns()
    row_pass(lt, 0)
    middle_exchange(0, True)

    def scale_0(i):
        v = jnp.exp2(row_m[i] - full_row(0, i))
        row_a[i] = v
        return v

    weigh(lt, scale_0, 0)
    refresh(c1, cen, False)
    for s in strips:
        m = jnp.sum(mass[s, :], axis=1, keepdims=True)
        ratio_j[s, :] = jnp.broadcast_to(2.0**log_ratio / m, (strip, LANES))

    def row_sums(i, _):
        part_sum = fold(
            jnp.add,
            [sub8(jnp.add, lt[i, s, :] * tile_lanes(ratio_j[s, :], blk)) for s in strips],
        )
        put_chunks(1, i, jnp.sum(part_sum, axis=0, keepdims=True) * row_a[i])
        return 0

    lax.fori_loop(0, nb, row_sums, 0)

    def second_scores(i, _):
        dot_scores(c1, i, lt2)
        return 0

    lax.fori_loop(0, nb // 2, second_scores, 0)
    middle_exchange(1, False)
    lax.fori_loop(nb // 2, nb, second_scores, 0)

    top[...] = jnp.full_like(top, -jnp.inf)
    tot[...] = jnp.zeros_like(tot)

    def second_columns(i, _):
        t = full_row(1, i)
        row_b[i] = row_a[i] / t
        pot = -full_row(0, i) - jnp.log2(t)
        for s in strips:
            online(lt2[i, s, :] + pot, s)
        return 0

    for h in range(2):
        end_exchange(1, h)
        lax.fori_loop(h * nb // 2, (h + 1) * nb // 2, second_columns, 0)
    finish_columns()
    row_pass(lt2, 2)
    middle_exchange(2, True)
    weigh(lt, lambda i: row_b[i])
    refresh(previous, cen, True)
    weigh(lt2, lambda i: jnp.exp2(row_m[i] - full_row(2, i)), 2)
    refresh(newest, c1, False)
    for h in range(2):
        row_out[h] = -LN2 * full_row(2, 2 * d + h)
    list_out[...] = LN2 * cp[...].T[0:1, :]


def shards(n_dp, n_cent, points, centroids):
    rows, width = points.shape
    lists = centroids.shape[0]
    n = n_dp * n_cent
    blk = rows // 2
    nb = 2 * n_dp
    w_all = rows * n_dp // LANES
    f32, bf16 = jnp.float32, jnp.bfloat16
    dma = pltpu.SemaphoreType.DMA
    vmem = pl.BlockSpec(memory_space=pltpu.VMEM)
    newest, previous, row_pot, list_pot = pl.pallas_call(
        functools.partial(kernel, n_dp, n_cent),
        out_shape=(
            jax.ShapeDtypeStruct((lists, width), bf16),
            jax.ShapeDtypeStruct((lists, width), bf16),
            jax.ShapeDtypeStruct((2, 1, blk), f32),
            jax.ShapeDtypeStruct((1, lists), f32),
        ),
        in_specs=[pl.BlockSpec(memory_space=pl.ANY), vmem],
        out_specs=(vmem, vmem, vmem, vmem),
        scratch_shapes=[
            pltpu.VMEM((nb, blk, width), bf16),
            pltpu.VMEM((nb, lists, blk), f32),
            pltpu.VMEM((nb, lists, blk), f32),
            pltpu.VMEM((lists, blk), bf16),
            pltpu.VMEM((lists, blk), bf16),
            pltpu.VMEM((lists, width), f32),
            pltpu.VMEM((lists, width), bf16),
            pltpu.VMEM((lists, LANES), f32),
            pltpu.VMEM((lists, LANES), f32),
            pltpu.VMEM((lists, LANES), f32),
            pltpu.VMEM((lists, LANES), f32),
            pltpu.VMEM((lists, LANES), f32),
            pltpu.VMEM((nb, 1, blk), f32),
            pltpu.VMEM((nb, 1, blk), f32),
            pltpu.VMEM((nb, 1, blk), f32),
            pltpu.VMEM((3, w_all, 1, LANES), f32),
            pltpu.VMEM((3, n, 1, LANES), f32),
            pltpu.VMEM((3, w_all, 1, LANES), f32),
            dma, pltpu.SemaphoreType.REGULAR((16,)), dma((14,)), dma((14,)), dma((13,)), dma((13,)),
            dma((3,)), dma((3,)), dma((3,)), dma((6,)),
        ],
        compiler_params=pltpu.CompilerParams(
            collective_id=0, has_side_effects=True, vmem_limit_bytes=52 * 1024 * 1024
        ),
    )(points.reshape(2, blk, width), centroids)
    return newest, previous, row_pot.reshape(rows), list_pot.reshape(lists)


def solution(mesh):
    return jax.shard_map(
        functools.partial(shards, mesh.shape["dp"], mesh.shape["cent"]),
        mesh=mesh,
        in_specs=(P("dp", None), P(("cent", "dp"), None)),
        out_specs=(P(("cent", "dp"), None), P(("cent", "dp"), None), P("dp"), P(("cent", "dp"))),
        check_vma=False,
    )
```
